256 devices in a mesh: row: 8 (over y, core), col: 32 (over x, z).
Axes of the slice: x: 4, y: 4, z: 8, core: 2. Of those that a mesh axis runs over, the one named last changes fastest.
Arguments:
- features: bfloat16 [65536, 256], P(('col', 'row')), may hold values from -6 to 6
- weight: bfloat16 [256, 256], replicated, may hold values from -0.375 to 0.375
- tile_coords: int32 [8, 32, 144, 2], P('row', 'col'), may hold values from 0 to 63, as said below
- tile_live: int32 [8, 32], P('row', 'col'), may hold values from 36 to 144, as said below
- tile_edges: int32 [8, 32, 144, 128, 128], P('row', 'col'), may hold values 0 or 1
- row_degree: int32 [65536], P(('row', 'col')), may hold values from 1 to 64
- col_degree: int32 [65536], P(('col', 'row')), may hold values from 1 to 64
- cotangent: bfloat16 [65536, 256], P(('row', 'col')), may hold values from -6 to 6
Outputs:
- aggregated: bfloat16 [65536, 256], P(('row', 'col'))
- grad_features: bfloat16 [65536, 256], P(('col', 'row'))
- grad_weight: float32 [256, 256], replicated
The draws below stay inside these ranges and needn't reach their ends.
Inputs may be any that keep to these rules, and one draw needn't show every extreme that they name: `tile_coords`: entry 0 of a slot is a row tile of the block, 0 to 63, entry 1 a column tile, 0 to 15; slots naming the same position add. `tile_live`: the number of live leading slots of each block's list; some block fills all 144 slots.
All inputs are finite; a program needn't handle non-finite values. No bound on the sum of `tile_edges` on one device may be relied on, other than what follows from the above.
Results may differ from the reference program's by a relative error of at most 0.0055.
Values may be sent and summed in bfloat16 or wider, within the bound.
No kernel may reach another device: no remote copies, remote signals or barrier semaphores. Data moves between devices by JAX's collectives and lax.ppermute only.
A program may use at most 128 MiB of HBM per device.

```python
import jax
import jax.numpy as jnp
from jax import lax

F = 256
TILE = 128
COL_TILES = 16
TILES_DEV = 144
NODES = 65536
ROW_TILES = 64
N_ROW = 8
N_COL = 32


def draw_tile_coords(key, part):
    key = jax.random.fold_in(key, 11)
    first_key, second_key = jax.random.split(key)
    row_tiles = jax.random.randint(first_key, (N_ROW, N_COL, TILES_DEV, 1), 0, ROW_TILES)
    col_tiles = jax.random.randint(second_key, (N_ROW, N_COL, TILES_DEV, 1), 0, COL_TILES)
    return jnp.concatenate([row_tiles, col_tiles], axis=3).astype(jnp.int32)


def draw_tile_live(key, part):
    key = jax.random.fold_in(key, 23)
    count_key, full_key, least_key = jax.random.split(key, 3)
    blocks = N_ROW * N_COL
    counts = jax.random.randint(count_key, (blocks,), TILES_DEV // 4, TILES_DEV + 1)
    full_at = jax.random.randint(full_key, (), 0, blocks)
    least_at = (full_at + 1 + jax.random.randint(least_key, (), 0, blocks - 1)) % blocks
    places = jnp.arange(blocks)
    counts = jnp.where(places == full_at, TILES_DEV, counts)
    counts = jnp.where(places == least_at, TILES_DEV // 4, counts)
    return counts.reshape(N_ROW, N_COL).astype(jnp.int32)


def plant(entries, key, smallest, largest):
    longest = entries.shape.index(max(entries.shape))
    spots = []
    for shift in (0, 1):
        where = [jax.random.randint(jax.random.fold_in(key, axis), (), 0, length) for axis, length in enumerate(entries.shape)]
        where[longest] = (where[longest] + shift) % entries.shape[longest]
        spots.append(tuple(where))
    return entries.at[spots[0]].set(smallest).at[spots[1]].set(largest)


def block_scale(key, shape, shards, low, high):
    level = 1.0
    for position, shards_of in shards:
        draws = jax.random.uniform(jax.random.fold_in(jax.random.fold_in(key, 6), position), (shards_of,), jnp.float32, low / len(shards), high / len(shards))
        level = level * jnp.repeat(jnp.exp(draws), shape[position] // shards_of).reshape((-1,) + (1,) * (len(shape) - 1 - position))
    return level


def gaussian(key, extent, spread, limit, cuts=(), held_as=jnp.bfloat16):
    values = spread * jax.random.normal(key, extent, jnp.float32)
    if cuts:
        values = values * block_scale(key, extent, cuts, -0.22, 0.18)
    return jnp.clip(values, -limit, limit).astype(held_as)


def setup_inputs(seed: int = 0) -> dict:
    keys = jax.random.split(jax.random.key(seed), 9)
    features = gaussian(keys[0], (NODES, F), 1.0, 6.0, ((0, 256),))
    weight = gaussian(keys[1], (F, F), F ** -0.5, 0.375)
    tile_coords = draw_tile_coords(jax.random.fold_in(keys[8], 71), 0)
    tile_live = draw_tile_live(jax.random.fold_in(keys[8], 71), 0)
    tile_edges = plant((jax.random.randint(keys[4], (N_ROW, N_COL, TILES_DEV, TILE, TILE), 0, 32) < 1).astype(jnp.int32), jax.random.fold_in(keys[4], 1), 0, 1)
    row_degree = plant(jax.random.randint(keys[5], (NODES,), 1, 65), jax.random.fold_in(keys[5], 1), 1, 64).astype(jnp.int32)
    col_degree = plant(jax.random.randint(keys[6], (NODES,), 1, 65), jax.random.fold_in(keys[6], 1), 1, 64).astype(jnp.int32)
    cotangent = gaussian(keys[7], (NODES, F), 1.0, 6.0, ((0, 256),))
    return dict(features=features, weight=weight, tile_coords=tile_coords, tile_live=tile_live, tile_edges=tile_edges, row_degree=row_degree, col_degree=col_degree, cotangent=cotangent)


def reference(features, weight, tile_coords, tile_live, tile_edges, row_degree, col_degree, cotangent):
    row_scale = lax.rsqrt(row_degree.astype(jnp.float32))
    col_scale = lax.rsqrt(col_degree.astype(jnp.float32))
    panel = (col_scale[:, None] * jnp.dot(features, weight, preferred_element_type=jnp.float32)).astype(jnp.bfloat16)
    panel_tiles = panel.reshape(NODES // TILE, TILE, F).astype(jnp.float32)
    slot_ids = jnp.arange(TILES_DEV, dtype=jnp.int32)

    def block_edges(device):
        row_block = device // N_COL
        col_block = device % N_COL
        coords = tile_coords[row_block, col_block]
        valid_slots = slot_ids < tile_live[row_block, col_block]
        local_edges = jnp.where(valid_slots[:, None, None], tile_edges[row_block, col_block], 0).astype(jnp.float32)
        rows_global = (row_block * ROW_TILES + coords[:, 0]).astype(jnp.int32)
        cols_global = (col_block * COL_TILES + coords[:, 1]).astype(jnp.int32)
        return (local_edges, rows_global, cols_global)

    def forward_step(totals, device):
        local_edges, rows_global, cols_global = block_edges(device)
        picked = panel_tiles[cols_global]
        products = jnp.einsum('sij,sjf->sif', local_edges, picked, precision=lax.Precision.HIGHEST)
        return (totals.at[rows_global].add(products), None)
    devices = jnp.arange(N_ROW * N_COL, dtype=jnp.int32)
    zeros_tiles = jnp.zeros((NODES // TILE, TILE, F), jnp.float32)
    summed, _ = lax.scan(forward_step, zeros_tiles, devices)
    aggregated = (row_scale[:, None] * summed.reshape(NODES, F)).astype(jnp.bfloat16)
    upstream = (row_scale[:, None] * cotangent.astype(jnp.float32)).astype(jnp.bfloat16)
    upstream_tiles = upstream.reshape(NODES // TILE, TILE, F).astype(jnp.float32)

    def backward_step(totals, device):
        local_edges, rows_global, cols_global = block_edges(device)
        picked = upstream_tiles[rows_global]
        products = jnp.einsum('sji,sjf->sif', local_edges, picked, precision=lax.Precision.HIGHEST)
        return (totals.at[cols_global].add(products), None)
    back_summed, _ = lax.scan(backward_step, zeros_tiles, devices)
    grad_panel = (col_scale[:, None] * back_summed.reshape(NODES, F)).astype(jnp.bfloat16)
    grad_features = jnp.dot(grad_panel, weight.T, preferred_element_type=jnp.float32).astype(jnp.bfloat16)
    grad_weight = jnp.dot(features.T, grad_panel, preferred_element_type=jnp.float32)
    return (aggregated, grad_features, grad_weight)
```

```python
import functools

import jax
import jax.numpy as jnp
from jax import lax
from jax.experimental import pallas as pl
from jax.experimental.pallas import tpu as pltpu
from jax.sharding import PartitionSpec as P

X, Z = 4, 8
Y = 4
CHUNK = 16
GROUP = 4


def along_z(d):
    return [(x * Z + z, x * Z + (z + d) % Z) for x in range(X) for z in range(Z)]


def along_x(d):
    return [(x * Z + z, ((x + d) % X) * Z + z) for x in range(X) for z in range(Z)]


def along_y(d):
    return [(y * 2 + c, ((y + d) % Y) * 2 + c) for y in range(Y) for c in range(2)]


OTHER_CORE = [(r, r ^ 1) for r in range(2 * Y)]
Z_GROUPS = [[x * Z + z for z in range(Z)] for x in range(X)]


def send(value, axis, pairs):
    return lax.ppermute(value, axis, pairs)


def exchange_z(value):
    return lax.all_to_all(value, "col", 0, 0, axis_index_groups=Z_GROUPS)


def chunk_tiles(meta_ref, live, chunk, edges_ref, product_ref, visit):
    first = chunk * CHUNK
    count = jnp.minimum(live - first, CHUNK)

    @pl.loop(0, (count + GROUP - 1) // GROUP)
    def _(step):
        spots = []
        for k in range(GROUP):
            here = step * GROUP + k
            at = first + here
            tile = jnp.where(at < live, edges_ref[here], 0).astype(jnp.float32).astype(jnp.bfloat16)
            spots.append((meta_ref[0, at], meta_ref[1, at]))
            product_ref[k] = visit.product(tile, *spots[-1])
        for k in range(GROUP):
            visit.add(product_ref[k], *spots[k])


class Forward:
    def __init__(self, panel_ref, total_ref):
        self.panel_ref, self.total_ref = panel_ref, total_ref

    def product(self, tile, slot, column):
        return jnp.dot(tile, self.panel_ref[column], preferred_element_type=jnp.float32)

    def add(self, product, slot, column):
        self.total_ref[slot] += product


class Backward:
    def __init__(self, upstream_ref, total_ref):
        self.upstream_ref, self.total_ref = upstream_ref, total_ref

    def product(self, tile, slot, column):
        return lax.dot_general(
            tile, self.upstream_ref[slot], (((0,), (0,)), ((), ())),
            preferred_element_type=jnp.float32,
        )

    def add(self, product, slot, column):
        self.total_ref[column] += product


def forward_kernel(
    meta_ref, live_ref, edges_ref, panel_ref,
    x_up_ref, x_down_ref, x_up_later_ref, x_down_later_ref, x_own_ref,
    z_up_ref, z_down_ref, z_later_ref,
    total, products,
):
    chunk = pl.program_id(0)
    live = live_ref[0]

    @pl.when(chunk == 0)
    def _():
        total[...] = jnp.zeros_like(total)

    @pl.when(chunk * CHUNK < live)
    def _():
        chunk_tiles(meta_ref, live, chunk, edges_ref, products, Forward(panel_ref, total))

    @pl.when(chunk == pl.num_programs(0) - 1)
    def _():
        bf16 = jnp.bfloat16
        for z in range(4):
            x_up_ref[z] = total[16 + z].astype(bf16)
            x_up_ref[4 + z] = total[8 + 4 + z].astype(bf16)
            x_down_ref[z] = total[24 + z].astype(bf16)
            x_down_ref[4 + z] = total[16 + 4 + z].astype(bf16)
            x_up_later_ref[z] = total[8 + z]
            x_down_later_ref[z] = total[24 + 4 + z]
        for z in range(8):
            x_own_ref[z] = total[z]
        for d in range(2):
            z_up_ref[d] = total[32 + 16 + d].astype(bf16)
            z_down_ref[d] = total[32 + 16 + 2 + d].astype(bf16)
        for k, dz in enumerate((3, 5, 2, 6, 1, 7, 0)):
            for d in range(4):
                z_later_ref[k, d] = total[32 + dz * 4 + d]


def backward_kernel(places, meta_ref, live_ref, edges_ref, *refs):
    pieces = refs[: len(places)]
    total_ref, upstream, products, sems = refs[len(places) :]
    chunk = pl.program_id(0)
    live = live_ref[0]

    @pl.when(chunk == 0)
    def _():
        copies = [
            pltpu.make_async_copy(piece, upstream.at[pl.ds(at, piece.shape[0])], sems.at[k])
            for k, (piece, at) in enumerate(zip(pieces, places))
        ]
        for copy in copies:
            copy.start()
        total_ref[...] = jnp.zeros_like(total_ref)
        for copy in copies:
            copy.wait()

    @pl.when(chunk * CHUNK < live)
    def _():
        chunk_tiles(meta_ref, live, chunk, edges_ref, products, Backward(upstream, total_ref))


def edges_spec(size):
    return pl.BlockSpec(
        (CHUNK, size, size),
        lambda i, meta, live: (jnp.minimum(i, (live[0] - 1) // CHUNK), 0, 0),
    )


def whole(shape):
    return pl.BlockSpec(shape, lambda i, meta, live: (0,) * len(shape))


PARAMS = dict(vmem_limit_bytes=48 * 1024 * 1024)


def forward(meta, live, edges, panel):
    slots, size, _ = edges.shape
    width = panel.shape[-1]
    f32, bf16 = jnp.float32, jnp.bfloat16
    outs = [
        ((8, size, width), bf16), ((8, size, width), bf16),
        ((4, size, width), f32), ((4, size, width), f32), ((8, size, width), f32),
        ((2, size, width), bf16), ((2, size, width), bf16), ((7, 4, size, width), f32),
    ]
    return pl.pallas_call(
        forward_kernel,
        grid_spec=pltpu.PrefetchScalarGridSpec(
            num_scalar_prefetch=2,
            grid=(slots // CHUNK,),
            in_specs=[edges_spec(size), whole(panel.shape)],
            out_specs=[whole(shape) for shape, _ in outs],
            scratch_shapes=[
                pltpu.VMEM((64, size, width), f32),
                pltpu.VMEM((GROUP, size, width), f32),
            ],
        ),
        out_shape=[jax.ShapeDtypeStruct(shape, dtype) for shape, dtype in outs],
        compiler_params=pltpu.CompilerParams(**PARAMS),
        cost_estimate=pl.CostEstimate(flops=10**10, bytes_accessed=2 * 10**7, transcendentals=0),
        name="forward_tiles",
    )(meta, live, edges, panel)


def backward(meta, live, edges, pieces, places, col_tiles):
    slots, size, _ = edges.shape
    width = pieces[0].shape[-1]
    f32 = jnp.float32
    return pl.pallas_call(
        functools.partial(backward_kernel, places),
        grid_spec=pltpu.PrefetchScalarGridSpec(
            num_scalar_prefetch=2,
            grid=(slots // CHUNK,),
            in_specs=[edges_spec(size)] + [pl.BlockSpec(memory_space=pl.ANY)] * len(pieces),
            out_specs=whole((col_tiles, size, width)),
            scratch_shapes=[
                pltpu.VMEM((64, size, width), jnp.bfloat16),
                pltpu.VMEM((GROUP, size, width), f32),
                pltpu.SemaphoreType.DMA((len(pieces),)),
            ],
        ),
        out_shape=jax.ShapeDtypeStruct((col_tiles, size, width), f32),
        compiler_params=pltpu.CompilerParams(**PARAMS),
        cost_estimate=pl.CostEstimate(flops=10**10, bytes_accessed=2 * 10**7, transcendentals=0),
        name="backward_tiles",
    )(meta, live, edges, *pieces)


def gather_col(own, size):
    first, second = own[:size], own[size:]
    z_all = exchange_z(jnp.broadcast_to(first, (Z,) + first.shape))
    x_all = jnp.stack(
        [
            second,
            send(second, "col", along_x(-1)),
            send(second, "col", along_x(2)),
            send(second, "col", along_x(1)),
        ]
    )
    places = [(z_all, 0), (x_all, 32)]
    left = send(z_all, "col", along_x(1))
    right = send(z_all, "col", along_x(-1))
    places += [(left, 24), (right, 8)]
    places += [
        (send(left[:4], "col", along_x(1)), 16),
        (send(right[4:], "col", along_x(-1)), 20),
    ]
    up = down = x_all
    for k in range(1, 4):
        up = send(up, "col", along_z(1))
        down = send(down, "col", along_z(-1))
        places += [(up, 32 + 4 * (8 - k)), (down, 32 + 4 * k)]
    places += [
        (send(up[:2], "col", along_z(1)), 32 + 16),
        (send(down[2:], "col", along_z(-1)), 32 + 18),
    ]
    return [piece for piece, _ in places], [at for _, at in places]


def scatter_col(parts):
    x_up, x_down, x_up_later, x_down_later, x_own, z_up, z_down, z_later = parts
    f32, bf16 = jnp.float32, jnp.bfloat16
    from_left = send(x_up, "col", along_x(1))
    from_right = send(x_down, "col", along_x(-1))
    from_below = send(z_up, "col", along_z(1))
    from_above = send(z_down, "col", along_z(-1))

    up = z_later[0] + jnp.concatenate([from_below, jnp.zeros_like(from_below)]).astype(f32)
    down = z_later[1] + jnp.concatenate([jnp.zeros_like(from_above), from_above]).astype(f32)
    up, down = up.astype(bf16), down.astype(bf16)
    for k in (2, 4):
        from_below = send(up, "col", along_z(1))
        from_above = send(down, "col", along_z(-1))
        up = (z_later[k] + from_below.astype(f32)).astype(bf16)
        down = (z_later[k + 1] + from_above.astype(f32)).astype(bf16)
    from_below = send(up, "col", along_z(1))
    from_above = send(down, "col", along_z(-1))
    column = z_later[6] + from_below.astype(f32) + from_above.astype(f32)
    packed = column.astype(bf16)
    second = column[0] + sum(
        send(packed[d], "col", along_x(d)).astype(f32) for d in range(1, X)
    )

    last_left = send((x_up_later + from_left[:4].astype(f32)).astype(bf16), "col", along_x(1))
    last_right = send((x_down_later + from_right[4:].astype(f32)).astype(bf16), "col", along_x(-1))
    plane = (
        x_own
        + jnp.concatenate([last_left, from_left[4:]]).astype(f32)
        + jnp.concatenate([from_right[:4], last_right]).astype(f32)
    )
    first = jnp.sum(exchange_z(plane.astype(bf16)).astype(f32), axis=0)
    return jnp.concatenate([first, second])


def sum_all(terms):
    rows, width = terms.shape
    y, core = lax.axis_index("row") // 2, lax.axis_index("row") % 2
    blocks = terms.reshape(2, rows // 2, width)
    own = lax.dynamic_index_in_dim(blocks, core, 0, False)
    other = lax.dynamic_index_in_dim(blocks, 1 - core, 0, False)
    half = own + send(other, "row", OTHER_CORE)
    quarters = half.reshape(Y, rows // 2 // Y, width)

    def quarter(d):
        return lax.dynamic_index_in_dim(quarters, (y + d) % Y, 0, False)

    part = quarter(0) + sum(send(quarter(d), "row", along_y(d)) for d in range(1, Y))
    part = jnp.sum(exchange_z(jnp.broadcast_to(part, (Z,) + part.shape)), axis=0)
    arrived = [send(part, "col", along_x(d)) for d in range(1, X)]
    ordered = [part] + arrived
    x = lax.axis_index("col") // Z
    stacked = jnp.stack(ordered)
    part = jnp.sum(
        jnp.take(stacked, (x - jnp.arange(X, dtype=jnp.int32)) % X, axis=0), axis=0
    )
    got = jnp.stack([part] + [send(part, "row", along_y(d)) for d in range(1, Y)])
    half = jnp.take(got, (y - jnp.arange(Y, dtype=jnp.int32)) % Y, axis=0)
    half = half.reshape(rows // 2, width)
    other = send(half, "row", OTHER_CORE)
    return jnp.where(
        core == 0, jnp.concatenate([half, other]), jnp.concatenate([other, half])
    )


def shards(features, weight, tile_coords, tile_live, tile_edges, row_degree, col_degree, cotangent):
    f32, bf16 = jnp.float32, jnp.bfloat16
    size = tile_edges.shape[-1]
    nodes, width = features.shape
    row_scale = lax.rsqrt(row_degree.astype(f32))
    col_scale = lax.rsqrt(col_degree.astype(f32))
    coords = tile_coords[0, 0]
    live = tile_live[0]
    edges = tile_edges[0, 0]

    col = lax.axis_index("col")
    owner, half = coords[:, 0] // 2, coords[:, 0] % 2
    dx = (owner // Z - col // Z) % X
    dz = (owner % Z - col % Z) % Z
    slot = jnp.where(half == 0, dx * Z + owner % Z, 32 + dz * X + dx)
    meta = jnp.stack([slot, coords[:, 1]]).astype(jnp.int32)

    upstream = (row_scale[:, None] * cotangent.astype(f32)).astype(bf16)
    pieces, places = gather_col(upstream, size)

    degrees = jnp.zeros((16, width), bf16).at[0].set(col_degree.astype(bf16))
    block = lax.all_gather(jnp.concatenate([features, degrees]), "row", axis=0)
    block_features = block[:, :nodes].reshape(-1, width)
    block_scale = lax.rsqrt(block[:, nodes].astype(f32)).reshape(-1, 1)
    panel = (
        block_scale * jnp.dot(block_features, weight, preferred_element_type=f32)
    ).astype(bf16)
    panel = panel.reshape(-1, size, width)

    parts = forward(meta, live, edges, panel)
    aggregated = (row_scale[:, None] * scatter_col(parts)).astype(bf16)

    back = backward(meta, live, edges, pieces, places, panel.shape[0]).reshape(-1, width)
    terms = lax.dot_general(
        block_features,
        (block_scale * back).astype(bf16),
        (((0,), (0,)), ((), ())),
        preferred_element_type=f32,
    )
    grad_weight = sum_all(terms)
    back_summed = lax.psum_scatter(back, "row", scatter_dimension=0, tiled=True)
    grad_panel = (col_scale[:, None] * back_summed).astype(bf16)
    grad_features = jnp.dot(grad_panel, weight.T, preferred_element_type=f32).astype(bf16)
    return aggregated, grad_features, grad_weight


def solution(mesh):
    in_specs = (
        P(("col", "row"), None),
        P(),
        P("row", "col", None, None),
        P("row", "col"),
        P("row", "col", None, None, None),
        P(("row", "col")),
        P(("col", "row")),
        P(("row", "col"), None),
    )
    out_specs = (P(("row", "col"), None), P(("col", "row"), None), P())
    return jax.shard_map(shards, mesh=mesh, in_specs=in_specs, out_specs=out_specs, check_vma=False)
```

```python
import functools

import jax
import jax.numpy as jnp
from jax import lax
from jax.experimental import pallas as pl
from jax.experimental.pallas import tpu as pltpu
from jax.sharding import PartitionSpec as P

X, Z = 4, 8
Y = 4
CHUNK = 16
GROUP = 8
VMEM_MIB = 60


def along_z(d):
    return [(x * Z + z, x * Z + (z + d) % Z) for x in range(X) for z in range(Z)]


def along_x(d):
    return [(x * Z + z, ((x + d) % X) * Z + z) for x in range(X) for z in range(Z)]


def along_y(d):
    return [(y * 2 + c, ((y + d) % Y) * 2 + c) for y in range(Y) for c in range(2)]


def by_core(along):
    return [
        (row * X * Z + a, row * X * Z + b)
        for row in range(2 * Y)
        for a, b in along(1 - 2 * (row % 2))
    ]


OTHER_CORE = [(r, r ^ 1) for r in range(2 * Y)]
Z_GROUPS = [[x * Z + z for z in range(Z)] for x in range(X)]
X_GROUPS = [[x * Z + z for x in range(X)] for z in range(Z)]


def send(value, axis, pairs):
    return lax.ppermute(value, axis, pairs)


def exchange_z(value):
    return lax.all_to_all(value, "col", 0, 0, axis_index_groups=Z_GROUPS)


def exchange_x(value):
    return lax.all_to_all(value, "col", 0, 0, axis_index_groups=X_GROUPS)


def scale_of(degrees):
    scale = lax.rsqrt(degrees.astype(jnp.float32))
    return jnp.transpose(jnp.broadcast_to(scale, (128,) + scale.shape[1:]))


def tile_sums(live, edges_hbm, edges, sems, totals, prepare, product, target):
    chunks = (live + CHUNK - 1) // CHUNK

    def load(chunk):
        part = pl.ds(chunk * CHUNK, CHUNK)
        return pltpu.make_async_copy(edges_hbm.at[part], edges.at[part], sems.at[chunk])

    @pl.loop(0, chunks)
    def _(chunk):
        load(chunk).start()

    for total in totals:
        total[...] = jnp.zeros_like(total)
    prepare()

    @pl.loop(0, chunks)
    def _(chunk):
        load(chunk).wait()
        count = jnp.minimum(live - chunk * CHUNK, CHUNK)

        @pl.loop(0, (count + GROUP - 1) // GROUP)
        def _(step):
            for k in range(GROUP):
                at = chunk * CHUNK + step * GROUP + k
                tile = jnp.where(at < live, edges[at], 0)
                value = product(tile.astype(jnp.float32).astype(jnp.bfloat16), at)
                slot = target(at)
                for half, total in enumerate(totals):
                    total[slot] += value[:, half * 128 : half * 128 + 128]


def forward_kernel(
    deps, meta_ref, scalars_ref, edges_hbm, own_ref, other_ref, weight_ref, *refs
):
    out_ref, panel, left, right, edges, sems = refs[deps:]
    live = scalars_ref[0]
    size = left.shape[1]

    def prepare():
        for block in range(2 * Y):
            ref, dy = (own_ref, other_ref)[block // Y], block % Y
            scale = scale_of(ref[dy, 2 * size :][:1])
            value = jnp.dot(
                ref[dy, : 2 * size], weight_ref[...], preferred_element_type=jnp.float32
            )
            value = value * jnp.concatenate([scale, scale], axis=1)
            panel[pl.ds(2 * block, 2)] = value.astype(jnp.bfloat16).reshape(2, size, -1)

    def product(tile, at):
        return jnp.dot(tile, panel[meta_ref[2, at]], preferred_element_type=jnp.float32)

    tile_sums(
        live, edges_hbm, edges, sems, (left, right), prepare, product,
        lambda at: meta_ref[0, at],
    )
    for slot in range(out_ref.shape[0]):
        out_ref[slot, :, :128] = left[slot].astype(jnp.bfloat16)
        out_ref[slot, :, 128:] = right[slot].astype(jnp.bfloat16)


def backward_kernel(
    places, deps, meta_ref, scalars_ref, edges_hbm, own_ref, other_ref, *refs
):
    pieces = refs[: len(places)]
    (keep_ref, far_ref, left, right, upstream, terms, edges, sems, piece_sems) = refs[
        len(places) + deps :
    ]
    live, row = scalars_ref[0], scalars_ref[1]
    size = left.shape[1]
    copies = [
        pltpu.make_async_copy(piece, upstream.at[pl.ds(at, piece.shape[0])], piece_sems.at[k])
        for k, (piece, at) in enumerate(zip(pieces, places))
    ]
    for copy in copies:
        copy.start()

    def prepare():
        for copy in copies:
            copy.wait()

    def product(tile, at):
        return lax.dot_general(
            tile, upstream[meta_ref[1, at]], (((0,), (0,)), ((), ())),
            preferred_element_type=jnp.float32,
        )

    tile_sums(
        live, edges_hbm, edges, sems, (left, right), prepare, product,
        lambda at: meta_ref[2, at],
    )
    y, core = row // 2, row % 2
    result = None
    for block in range(2 * Y):
        far, dy = block // Y, block % Y
        value = jnp.concatenate(
            [ref[pl.ds(2 * block, 2)].reshape(2 * size, 128) for ref in (left, right)], axis=1
        )
        if far:
            far_ref[dy, : 2 * size] = value.astype(jnp.bfloat16)
        else:
            keep_ref[dy, : 2 * size] = value
        ref = other_ref if far else own_ref
        scale = scale_of(ref[dy, 2 * size :][:1])
        scaled = (value * jnp.concatenate([scale, scale], axis=1)).astype(jnp.bfloat16)
        term = lax.dot_general(
            ref[dy, : 2 * size], scaled, (((0,), (0,)), ((), ())),
            preferred_element_type=jnp.float32,
        )
        result = term if result is None else result + term
    terms[...] = result.reshape(terms.shape)
    for block in range(2 * Y):
        far, dy = block // Y, block % Y
        value = terms[((y + dy) % Y) * 2 + (core + far) % 2]
        if far:
            far_ref[dy, 2 * size :] = value.astype(jnp.bfloat16)
        else:
            keep_ref[dy, 2 * size :] = value


PARAMS = dict(vmem_limit_bytes=VMEM_MIB * 1024 * 1024)
ANY = pl.BlockSpec(memory_space=pl.ANY)
VMEM = pl.BlockSpec(memory_space=pltpu.VMEM)
SMEM = pl.BlockSpec(memory_space=pltpu.SMEM)


def forward(meta, scalars, edges, own, other, weight, deps=()):
    slots, size, _ = edges.shape
    width = weight.shape[-1]
    f32, bf16 = jnp.float32, jnp.bfloat16
    return pl.pallas_call(
        functools.partial(forward_kernel, len(deps)),
        in_specs=[SMEM, SMEM, ANY, VMEM, VMEM, VMEM] + [ANY] * len(deps),
        out_specs=VMEM,
        scratch_shapes=[
            pltpu.VMEM((4 * Y, size, width), bf16),
            pltpu.VMEM((2 * X * Z, size, 128), f32),
            pltpu.VMEM((2 * X * Z, size, 128), f32),
            pltpu.VMEM(edges.shape, edges.dtype),
            pltpu.SemaphoreType.DMA((slots // CHUNK,)),
        ],
        out_shape=jax.ShapeDtypeStruct((2 * X * Z, size, width), bf16),
        compiler_params=pltpu.CompilerParams(**PARAMS),
        cost_estimate=pl.CostEstimate(flops=10**6, bytes_accessed=10**4, transcendentals=0),
        name="forward_tiles",
    )(meta, scalars, edges, own, other, weight, *deps)


def backward(meta, scalars, edges, own, other, pieces, places, deps):
    slots, size, _ = edges.shape
    width = pieces[0].shape[-1]
    rows = 2 * size + width // (2 * Y)
    f32, bf16 = jnp.float32, jnp.bfloat16
    outs = [((Y, rows, width), f32), ((Y, rows, width), bf16)]
    return pl.pallas_call(
        functools.partial(backward_kernel, places, len(deps)),
        in_specs=[SMEM, SMEM, ANY, VMEM, VMEM] + [ANY] * len(pieces + deps),
        out_specs=[VMEM] * len(outs),
        scratch_shapes=[
            pltpu.VMEM((4 * Y, size, 128), f32),
            pltpu.VMEM((4 * Y, size, 128), f32),
            pltpu.VMEM((2 * X * Z, size, width), bf16),
            pltpu.VMEM((2 * Y, width // (2 * Y), width), f32),
            pltpu.VMEM(edges.shape, edges.dtype),
            pltpu.SemaphoreType.DMA((slots // CHUNK,)),
            pltpu.SemaphoreType.DMA((len(pieces),)),
        ],
        out_shape=[jax.ShapeDtypeStruct(shape, dtype) for shape, dtype in outs],
        compiler_params=pltpu.CompilerParams(**PARAMS),
        cost_estimate=pl.CostEstimate(flops=10**6, bytes_accessed=10**4, transcendentals=0),
        name="backward_tiles",
    )(meta, scalars, edges, own, other, *pieces, *deps)


def gather_col(own, size, core):
    line = jnp.concatenate(
        [
            own,
            send(own, "col", along_x(-1)),
            send(own, "col", along_x(2)),
            send(own, "col", along_x(1)),
        ]
    ).reshape(2 * X, size, -1)
    places = [(line, 0)]
    up = down = line
    for k in range(1, 4):
        up = send(up, "col", along_z(1))
        down = send(down, "col", along_z(-1))
        places += [(up, 8 * (8 - k)), (down, 8 * k)]
    far = send(jnp.where(core == 0, up, down), ("row", "col"), by_core(along_z))
    places += [(far, 8 * 4)]
    return [piece for piece, _ in places], [at for _, at in places]


def gather_row(own):
    mine = jnp.stack(
        [
            own,
            send(own, "row", along_y(-1)),
            send(own, "row", along_y(2)),
            send(own, "row", along_y(1)),
        ]
    )
    return mine, send(mine, "row", OTHER_CORE)


def fold_cores_kernel(keep, recv, *outs):
    for d in range(Y):
        value = keep[d] + recv[d].astype(jnp.float32)
        outs[d][...] = value.astype(outs[d].dtype)


def scatter_row(keep, far):
    recv = send(far, "row", OTHER_CORE)
    shape = keep.shape[1:]
    own, *parts = pl.pallas_call(
        fold_cores_kernel,
        out_shape=[jax.ShapeDtypeStruct(shape, jnp.float32)]
        + [jax.ShapeDtypeStruct(shape, jnp.bfloat16)] * (Y - 1),
        name="fold_cores",
    )(keep, recv)
    return own + sum(
        send(part, "row", along_y(d)).astype(jnp.float32) for d, part in enumerate(parts, 1)
    )


def all_rows(value, y, core):
    got = jnp.stack([value] + [send(value, "row", along_y(d)) for d in range(1, Y)])
    mine = jnp.take(got, (y - jnp.arange(Y, dtype=jnp.int32)) % Y, axis=0)
    other = send(mine, "row", OTHER_CORE)
    pair = jnp.where(core == 0, jnp.stack([mine, other], 1), jnp.stack([other, mine], 1))
    return pair.reshape(-1, value.shape[-1])


def sum_col(value, bits):
    for bit in bits:
        value = value + send(value, "col", [(a, a ^ bit) for a in range(X * Z)])
    return value


def shards(features, weight, tile_coords, tile_live, tile_edges, row_degree, col_degree, cotangent):
    f32, bf16 = jnp.float32, jnp.bfloat16
    size = tile_edges.shape[-1]
    nodes, width = features.shape
    row_scale = lax.rsqrt(row_degree.astype(f32))
    col_scale = lax.rsqrt(col_degree.astype(f32))
    coords = tile_coords[0, 0]
    edges = tile_edges[0, 0]
    row, col = lax.axis_index("row"), lax.axis_index("col")
    y, core = row // 2, row % 2

    upstream = (row_scale[:, None] * cotangent.astype(f32)).astype(bf16)
    pieces, places = gather_col(upstream, size, core)

    degrees = jnp.zeros((16, width), bf16).at[0].set(col_degree.astype(bf16))
    mine, other = gather_row(jnp.concatenate([features, degrees]))

    owner, half = coords[:, 0] // 2, coords[:, 0] % 2
    dx = (owner // Z - col // Z) % X
    dz = (owner % Z - col % Z) % Z
    back_row = (dz * X + dx) * 2 + half
    col_owner, half = coords[:, 1] // 2, coords[:, 1] % 2
    column = ((col_owner + core) % 2 * Y + (col_owner // 2 - y) % Y) * 2 + half
    meta = jnp.stack([coords[:, 0], back_row, column]).astype(jnp.int32)
    scalars = jnp.stack([tile_live[0, 0], row]).astype(jnp.int32)

    first = forward(meta, scalars, edges, mine, other, weight, pieces[:1])
    first, *pieces[1:3] = lax.optimization_barrier((first, *pieces[1:3]))
    from_x = exchange_x(first.reshape(X, Z * nodes, width))
    from_x, pieces[-1] = lax.optimization_barrier((from_x, pieces[-1]))
    plane = jnp.sum(from_x.astype(f32), axis=0).astype(bf16)
    from_z = exchange_z(plane.reshape(Z, nodes, width))
    keep, far = backward(meta, scalars, edges, mine, other, pieces, places, [plane])
    back = scatter_row(keep, far)
    terms = sum_col(back[nodes:], (Z, 2 * Z))
    terms, from_z = lax.optimization_barrier((terms, from_z))
    grad_weight = all_rows(sum_col(terms, (1, 2, 4)), y, core)

    summed = jnp.sum(from_z.astype(f32), axis=0)
    aggregated = (row_scale[:, None] * summed).astype(bf16)

    grad_panel = (col_scale[:, None] * back[:nodes]).astype(bf16)
    grad_features = jnp.dot(grad_panel, weight.T, preferred_element_type=f32).astype(bf16)
    return aggregated, grad_features, grad_weight


def solution(mesh):
    in_specs = (
        P(("col", "row"), None),
        P(),
        P("row", "col", None, None),
        P("row", "col"),
        P("row", "col", None, None, None),
        P(("row", "col")),
        P(("col", "row")),
        P(("row", "col"), None),
    )
    out_specs = (P(("row", "col"), None), P(("col", "row"), None), P())
    return jax.shard_map(shards, mesh=mesh, in_specs=in_specs, out_specs=out_specs, check_vma=False)
```

```python
import functools

import jax
import jax.numpy as jnp
from jax import lax
from jax.experimental import pallas as pl
from jax.experimental.pallas import tpu as pltpu
from jax.sharding import PartitionSpec as P

X, Z = 4, 8
Y = 4
GROUP = 16
CHUNK = 16
VMEM_MIB = 60
FORWARD_ROW, BACK_ROW, COLUMN, ORDER = range(4)
FAR_X = X // 2
Z_ORDER = (Z // 2, 3, 5, 2, 6, 1, 7, 0)


def along_z(d):
    return [(x * Z + z, x * Z + (z + d) % Z) for x in range(X) for z in range(Z)]


def along_x(d):
    return [(x * Z + z, ((x + d) % X) * Z + z) for x in range(X) for z in range(Z)]


def along_y(d):
    return [(y * 2 + c, ((y + d) % Y) * 2 + c) for y in range(Y) for c in range(2)]


def by_core(along):
    return [
        (row * X * Z + a, row * X * Z + b)
        for row in range(2 * Y)
        for a, b in along(1 - 2 * (row % 2))
    ]


OTHER_CORE = [(r, r ^ 1) for r in range(2 * Y)]
Z_GROUPS = [[x * Z + z for z in range(Z)] for x in range(X)]


def send(value, axis, pairs):
    return lax.ppermute(value, axis, pairs)


def exchange_z(value):
    return lax.all_to_all(value, "col", 0, 0, axis_index_groups=Z_GROUPS)


def scale_of(degrees):
    scale = lax.rsqrt(degrees.astype(jnp.float32))
    return jnp.transpose(jnp.broadcast_to(scale, (128,) + scale.shape[1:]))


def load_all(live, edges_hbm, edges, sems):
    def load(chunk):
        part = pl.ds(chunk * CHUNK, CHUNK)
        return pltpu.make_async_copy(edges_hbm.at[part], edges.at[part], sems.at[chunk])

    @pl.loop(0, (live + CHUNK - 1) // CHUNK)
    def _(chunk):
        load(chunk).start()

    return lambda chunk: load(chunk).wait()


def add_tiles(begin, end, tile_of, product, target, totals):
    @pl.loop(0, (end - begin + GROUP - 1) // GROUP)
    def _(step):
        for k in range(GROUP):
            at = begin + step * GROUP + k
            value = product(tile_of(at).astype(jnp.float32).astype(jnp.bfloat16), at)
            slot = target(at)
            for half, total in enumerate(totals):
                total[slot] += value[:, half * 128 : half * 128 + 128]


def add_chunks(live, wait, tile_of, product, target, totals):
    @pl.loop(0, (live + CHUNK - 1) // CHUNK)
    def _(chunk):
        wait(chunk)
        begin = chunk * CHUNK
        add_tiles(begin, jnp.minimum(live, begin + CHUNK), tile_of, product, target, totals)


def forward_kernel(
    deps, meta_ref, scalars_ref, edges_hbm, own_ref, other_ref, weight_ref, *refs
):
    out_refs = refs[deps : deps + Z]
    panel, left, right, edges, sems = refs[deps + Z :]
    live = scalars_ref[0]
    size = left.shape[1]

    wait = load_all(live, edges_hbm, edges, sems)
    for total in (left, right):
        total[...] = jnp.zeros_like(total)
    for block in range(2 * Y):
        ref, dy = (own_ref, other_ref)[block // Y], block % Y
        scale = scale_of(ref[dy, 2 * size :][:1])
        value = jnp.dot(
            ref[dy, : 2 * size], weight_ref[...], preferred_element_type=jnp.float32
        )
        value = value * jnp.concatenate([scale, scale], axis=1)
        panel[pl.ds(2 * block, 2)] = value.astype(jnp.bfloat16).reshape(2, size, -1)

    def product(tile, at):
        return jnp.dot(tile, panel[meta_ref[COLUMN, at]], preferred_element_type=jnp.float32)

    add_chunks(
        live, wait, lambda at: jnp.where(at < live, edges[at], 0), product,
        lambda at: meta_ref[FORWARD_ROW, at], (left, right),
    )
    for out_ref, dz in zip(out_refs, Z_ORDER):
        for slot in range(2 * X):
            out_ref[slot, :, :128] = left[dz * 2 * X + slot].astype(jnp.bfloat16)
            out_ref[slot, :, 128:] = right[dz * 2 * X + slot].astype(jnp.bfloat16)


def back_product(upstream, tile, slot):
    return lax.dot_general(
        tile, upstream[slot], (((0,), (0,)), ((), ())), preferred_element_type=jnp.float32
    )


def backward_near_kernel(base, places, meta_ref, scalars_ref, edges_hbm, *refs):
    pieces = refs[: len(places)]
    own_hbm, other_hbm, left, right, features_ref, token_ref = refs[len(places) : len(places) + 6]
    own_ref, other_ref, upstream, edges, sems, piece_sems = refs[len(places) + 6 :]
    token_ref[...] = jnp.zeros_like(token_ref)
    live = scalars_ref[0]
    copies = [
        pltpu.make_async_copy(piece, upstream.at[pl.ds(at, piece.shape[0])], piece_sems.at[k])
        for k, (piece, at) in enumerate(zip(pieces, places))
    ]
    for k, (src, dst) in enumerate([(own_hbm, own_ref), (other_hbm, other_ref)], len(places)):
        copies.append(pltpu.make_async_copy(src, dst, piece_sems.at[k]))
    for copy in copies:
        copy.start()
    wait = load_all(live, edges_hbm, edges, sems)
    for total in (left, right):
        total[...] = jnp.zeros_like(total)
    for copy in copies:
        copy.wait()
    nodes = 2 * left.shape[1]
    for block in range(2 * Y):
        ref, dy = (own_ref, other_ref)[block // Y], block % Y
        scale = scale_of(ref[dy, nodes:][:1])
        scaled = ref[dy, :nodes].astype(jnp.float32) * jnp.concatenate([scale, scale], axis=1)
        features_ref[block] = jnp.transpose(scaled).astype(jnp.bfloat16)

    def here(at):
        row = meta_ref[BACK_ROW, at]
        return jnp.logical_and(at < live, jnp.logical_or(row < base, row >= base + 2 * Z))

    add_chunks(
        live, wait, lambda at: jnp.where(here(at), edges[at], 0),
        lambda tile, at: back_product(
            upstream, tile, jnp.where(here(at), meta_ref[BACK_ROW, at], 0)
        ),
        lambda at: meta_ref[COLUMN, at], (left, right),
    )


def backward_far_kernel(
    base, meta_ref, scalars_ref, edges_hbm, piece, near_left, near_right, features_hbm, _,
    keep_ref, far_ref, terms_keep_ref, terms_far_ref,
    left, right, upstream, features_ref, terms, edges, sems, input_sems,
):
    row, count = scalars_ref[1], scalars_ref[2]
    size = left.shape[1]
    pairs = [
        (piece, upstream), (near_left, left), (near_right, right),
        (features_hbm, features_ref),
    ]
    copies = [
        pltpu.make_async_copy(src, dst, input_sems.at[k]) for k, (src, dst) in enumerate(pairs)
    ]

    def load(at):
        return pltpu.make_async_copy(edges_hbm.at[meta_ref[ORDER, at]], edges.at[at], sems.at[at])

    for copy in copies[:3]:
        copy.start()

    @pl.loop(0, count)
    def _(at):
        load(at).start()

    for copy in copies[3:]:
        copy.start()
    for copy in copies[:3]:
        copy.wait()

    @pl.loop(0, count)
    def _(at):
        load(at).wait()

    def number(name, at):
        return meta_ref[name, meta_ref[ORDER, at]]

    add_tiles(
        0, count, lambda at: jnp.where(at < count, edges[at], 0),
        lambda tile, at: back_product(
            upstream, tile, jnp.where(at < count, number(BACK_ROW, at) - base, 0)
        ),
        lambda at: number(COLUMN, at), (left, right),
    )
    for copy in copies[3:]:
        copy.wait()
    y, core = row // 2, row % 2
    result = None
    for block in range(2 * Y):
        far, dy = block // Y, block % Y
        part = pl.ds(2 * block, 2)
        value = jnp.concatenate(
            [
                ref[part].reshape(2 * size, 128) for ref in (left, right)
            ],
            axis=1,
        )
        if far:
            far_ref[dy] = value.astype(jnp.bfloat16)
        else:
            keep_ref[dy] = value
        term = jnp.dot(
            features_ref[block], value.astype(jnp.bfloat16), preferred_element_type=jnp.float32
        )
        result = term if result is None else result + term
    terms[...] = result.reshape(terms.shape)
    for block in range(2 * Y):
        far, dy = block // Y, block % Y
        value = terms[((y + dy) % Y) * 2 + (core + far) % 2]
        (terms_far_ref if far else terms_keep_ref)[dy] = value


PARAMS = dict(vmem_limit_bytes=VMEM_MIB * 1024 * 1024)
ANY = pl.BlockSpec(memory_space=pl.ANY)
VMEM = pl.BlockSpec(memory_space=pltpu.VMEM)
SMEM = pl.BlockSpec(memory_space=pltpu.SMEM)


def forward(meta, scalars, edges, own, other, weight, deps=()):
    slots, size, _ = edges.shape
    width = weight.shape[-1]
    f32, bf16 = jnp.float32, jnp.bfloat16
    return pl.pallas_call(
        functools.partial(forward_kernel, len(deps)),
        in_specs=[SMEM, SMEM, ANY, VMEM, VMEM, VMEM] + [ANY] * len(deps),
        out_specs=[VMEM] * Z,
        scratch_shapes=[
            pltpu.VMEM((4 * Y, size, width), bf16),
            pltpu.VMEM((2 * X * Z, size, 128), f32),
            pltpu.VMEM((2 * X * Z, size, 128), f32),
            pltpu.VMEM(edges.shape, edges.dtype),
            pltpu.SemaphoreType.DMA((slots // CHUNK,)),
        ],
        out_shape=[jax.ShapeDtypeStruct((2 * X, size, width), bf16)] * Z,
        compiler_params=pltpu.CompilerParams(**PARAMS),
        cost_estimate=pl.CostEstimate(flops=10**6, bytes_accessed=10**4, transcendentals=0),
        name="forward_tiles",
    )(meta, scalars, edges, own, other, weight, *deps)


def backward_near(meta, scalars, edges, pieces, places, base, own, other):
    slots, size, _ = edges.shape
    width = pieces[0].shape[-1]
    f32, bf16 = jnp.float32, jnp.bfloat16
    return pl.pallas_call(
        functools.partial(backward_near_kernel, base, places),
        in_specs=[SMEM, SMEM, ANY] + [ANY] * (len(pieces) + 2),
        out_specs=[VMEM] * 4,
        scratch_shapes=[
            pltpu.VMEM(own.shape, bf16),
            pltpu.VMEM(other.shape, bf16),
            pltpu.VMEM((2 * X * Z, size, width), bf16),
            pltpu.VMEM(edges.shape, edges.dtype),
            pltpu.SemaphoreType.DMA((slots // CHUNK,)),
            pltpu.SemaphoreType.DMA((len(pieces) + 2,)),
        ],
        out_shape=[jax.ShapeDtypeStruct((4 * Y, size, 128), f32)] * 2
        + [
            jax.ShapeDtypeStruct((2 * Y, width, 2 * size), bf16),
            jax.ShapeDtypeStruct((8, 128), f32),
        ],
        compiler_params=pltpu.CompilerParams(**PARAMS),
        cost_estimate=pl.CostEstimate(flops=10**6, bytes_accessed=10**4, transcendentals=0),
        name="backward_near",
    )(meta, scalars, edges, *pieces, own, other)


def backward_far(meta, scalars, edges, piece, place, left, right, features, after):
    slots, size, _ = edges.shape
    width = piece.shape[-1]
    rows = width // (2 * Y)
    f32, bf16 = jnp.float32, jnp.bfloat16
    outs = [((Y, 2 * size, width), f32), ((Y, 2 * size, width), bf16)]
    outs += [((Y, rows, width), f32)] * 2
    return pl.pallas_call(
        functools.partial(backward_far_kernel, place),
        in_specs=[SMEM, SMEM] + [ANY] * 6,
        out_specs=[VMEM] * len(outs),
        scratch_shapes=[
            pltpu.VMEM((4 * Y, size, 128), f32),
            pltpu.VMEM((4 * Y, size, 128), f32),
            pltpu.VMEM(piece.shape, bf16),
            pltpu.VMEM(features.shape, bf16),
            pltpu.VMEM((2 * Y, rows, width), f32),
            pltpu.VMEM(edges.shape, edges.dtype),
            pltpu.SemaphoreType.DMA((slots,)),
            pltpu.SemaphoreType.DMA((4,)),
        ],
        out_shape=[jax.ShapeDtypeStruct(shape, dtype) for shape, dtype in outs],
        compiler_params=pltpu.CompilerParams(**PARAMS),
        cost_estimate=pl.CostEstimate(flops=10**6, bytes_accessed=10**4, transcendentals=0),
        name="backward_far",
    )(meta, scalars, edges, piece, left, right, features, after)


def gather_z(own, size, core):
    parts = {0: own}
    up = down = own
    for k in range(1, Z // 2):
        up, down = send(up, "col", along_z(1)), send(down, "col", along_z(-1))
        parts[Z - k], parts[k] = up, down
    parts[Z // 2] = send(jnp.where(core == 0, up, down), ("row", "col"), by_core(along_z))
    return jnp.concatenate([parts[k] for k in range(Z)]).reshape(2 * Z, size, -1)


def gather_x(plane, core):
    left = send(plane, "col", along_x(1))
    right = send(plane, "col", along_x(-1))
    far = send(jnp.where(core == 0, left, right), ("row", "col"), by_core(along_x))
    return [plane, left, right, far], [0, 3 * 2 * Z, 2 * Z, FAR_X * 2 * Z]


def gather_row(own):
    mine = jnp.stack(
        [
            own,
            send(own, "row", along_y(-1)),
            send(own, "row", along_y(2)),
            send(own, "row", along_y(1)),
        ]
    )
    return mine, send(mine, "row", OTHER_CORE)


def fold_cores_kernel(keep, recv, own, *outs):
    own[...] = keep[0] + recv[0].astype(jnp.float32)
    for d, out in enumerate(outs, 1):
        out[...] = (keep[d] + recv[d].astype(jnp.float32)).astype(out.dtype)


def scatter_row(keep, far):
    recv = send(far, "row", OTHER_CORE)
    shape = keep.shape[1:]
    own, *parts = pl.pallas_call(
        fold_cores_kernel,
        out_shape=[jax.ShapeDtypeStruct(shape, jnp.float32)]
        + [jax.ShapeDtypeStruct(shape, far.dtype)] * (Y - 1),
        name="fold_cores",
    )(keep, recv)
    return own + sum(
        send(part, "row", along_y(d)).astype(jnp.float32) for d, part in enumerate(parts, 1)
    )


def all_rows(value, y, core):
    mine = jnp.stack([value] + [send(value, "row", along_y(d)) for d in range(1, Y)])
    got = jnp.concatenate([mine, send(mine, "row", OTHER_CORE)])
    row = jnp.arange(2 * Y, dtype=jnp.int32)
    order = (row + core) % 2 * Y + (y - row // 2) % Y
    return jnp.take(got, order, axis=0).reshape(-1, value.shape[-1])


def scatter_start(far, first_up, first_down, core):
    f32, bf16 = jnp.float32, jnp.bfloat16
    recv = send(far, ("row", "col"), by_core(along_z)).astype(f32)
    up = (first_up.astype(f32) + jnp.where(core == 0, recv, 0)).astype(bf16)
    down = (first_down.astype(f32) + jnp.where(core == 0, 0, recv)).astype(bf16)
    return up, down


def scatter_round(up, down):
    return send(up, "col", along_z(1)), send(down, "col", along_z(-1))


def fold(received, own):
    return [(b.astype(jnp.float32) + a.astype(jnp.float32)).astype(a.dtype)
            for a, b in zip(received, own)]


def scatter_end(below, above, own):
    f32, bf16 = jnp.float32, jnp.bfloat16
    column = own.astype(f32) + below.astype(f32) + above.astype(f32)
    column = column.reshape(X, -1, column.shape[-1])
    return column[0] + sum(
        send(column[d].astype(bf16), "col", along_x(d)).astype(f32) for d in range(1, X)
    )


def sum_x(value, x):
    got = jnp.stack([value] + [send(value, "col", along_x(d)) for d in range(1, X)])
    order = (x - jnp.arange(X, dtype=jnp.int32)) % X
    return jnp.sum(jnp.take(got, order, axis=0), axis=0)


def sum_z(value):
    return jnp.sum(exchange_z(jnp.broadcast_to(value, (Z,) + value.shape)), axis=0)


def shards(features, weight, tile_coords, tile_live, tile_edges, row_degree, col_degree, cotangent):
    f32, bf16 = jnp.float32, jnp.bfloat16
    size = tile_edges.shape[-1]
    nodes, width = features.shape
    row_scale = lax.rsqrt(row_degree.astype(f32))
    col_scale = lax.rsqrt(col_degree.astype(f32))
    coords = tile_coords[0, 0]
    edges = tile_edges[0, 0]
    row, col = lax.axis_index("row"), lax.axis_index("col")
    y, core = row // 2, row % 2

    upstream = (row_scale[:, None] * cotangent.astype(f32)).astype(bf16)
    plane = gather_z(upstream, size, core)

    degrees = jnp.zeros((16, width), bf16).at[0].set(col_degree.astype(bf16))
    mine, other = gather_row(jnp.concatenate([features, degrees]))

    owner, half = coords[:, 0] // 2, coords[:, 0] % 2
    dx = (owner // Z - col // Z) % X
    dz = (owner % Z - col % Z) % Z
    forward_row = (dz * X + dx) * 2 + half
    back_row = (dx * Z + dz) * 2 + half
    col_owner, half = coords[:, 1] // 2, coords[:, 1] % 2
    column = ((col_owner + core) % 2 * Y + (col_owner // 2 - y) % Y) * 2 + half
    live = tile_live[0, 0]
    index = jnp.arange(coords.shape[0], dtype=jnp.int32)
    key = index + 256 * jnp.logical_or(index >= live, dx != FAR_X)
    place = jnp.sum(key[None, :] < key[:, None], axis=1)
    order = jnp.sum(jnp.where(place[:, None] == index, index[:, None], 0), axis=0)
    meta = jnp.stack([forward_row, back_row, column, order]).astype(jnp.int32)
    scalars = jnp.stack([live, row, jnp.sum(key < 256)]).astype(jnp.int32)

    far, *parts = forward(meta, scalars, edges, mine, other, weight)
    (plane, left, right, last), places = gather_x(plane, core)
    up, down = scatter_start(far, *parts[:2], core)
    up, down, left, right = lax.optimization_barrier((up, down, left, right))
    received = scatter_round(up, down)
    *sums, token = backward_near(
        meta, scalars, edges, [plane, left, right], places[:-1], places[-1], mine, other
    )
    up, down = fold(received, parts[2:4])
    up, down, token = lax.optimization_barrier((up, down, token))
    received = scatter_round(up, down)
    keep, far, terms_keep, terms_far = backward_far(
        meta, scalars, edges, last, places[-1], *sums, token
    )
    received = scatter_round(*fold(received, parts[4:6]))
    aggregated = (row_scale[:, None] * scatter_end(*received, parts[6])).astype(bf16)

    terms = terms_keep + send(terms_far, "row", OTHER_CORE)
    terms = terms[0] + sum(send(terms[d], "row", along_y(d)) for d in range(1, Y))
    terms = sum_x(terms, col // Z)
    grad_weight = all_rows(sum_z(terms), y, core)
    back = scatter_row(keep, far)
    grad_panel = (col_scale[:, None] * back).astype(bf16)
    grad_features = jnp.dot(grad_panel, weight.T, preferred_element_type=f32).astype(bf16)
    return aggregated, grad_features, grad_weight


def solution(mesh):
    in_specs = (
        P(("col", "row"), None),
        P(),
        P("row", "col", None, None),
        P("row", "col"),
        P("row", "col", None, None, None),
        P(("row", "col")),
        P(("col", "row")),
        P(("row", "col"), None),
    )
    out_specs = (P(("row", "col"), None), P(("col", "row"), None), P())
    return jax.shard_map(shards, mesh=mesh, in_specs=in_specs, out_specs=out_specs, check_vma=False)
```

```python
import functools

import jax
import jax.numpy as jnp
from jax import lax
from jax.experimental import pallas as pl
from jax.experimental.pallas import tpu as pltpu
from jax.sharding import PartitionSpec as P

X, Z = 4, 8
Y = 4
GROUP = 16
CHUNK = 16
VMEM_MIB = 60
FORWARD_ROW, BACK_ROW, COLUMN, ORDER = range(4)
FAR_X = X // 2
Z_ORDER = (Z // 2, 3, 5, 2, 6, 1, 7, 0)


def along_z(d):
    return [(x * Z + z, x * Z + (z + d) % Z) for x in range(X) for z in range(Z)]


def along_x(d):
    return [(x * Z + z, ((x + d) % X) * Z + z) for x in range(X) for z in range(Z)]


def along_y(d):
    return [(y * 2 + c, ((y + d) % Y) * 2 + c) for y in range(Y) for c in range(2)]


def by_core(along):
    return [
        (row * X * Z + a, row * X * Z + b)
        for row in range(2 * Y)
        for a, b in along(1 - 2 * (row % 2))
    ]


OTHER_CORE = [(r, r ^ 1) for r in range(2 * Y)]
Z_GROUPS = [[x * Z + z for z in range(Z)] for x in range(X)]


def send(value, axis, pairs):
    return lax.ppermute(value, axis, pairs)


def exchange_z(value):
    return lax.all_to_all(value, "col", 0, 0, axis_index_groups=Z_GROUPS)


def scale_of(degrees):
    scale = lax.rsqrt(degrees.astype(jnp.float32))
    return jnp.transpose(jnp.broadcast_to(scale, (128,) + scale.shape[1:]))


def load_all(live, edges_hbm, edges, sems):
    def load(chunk):
        part = pl.ds(chunk * CHUNK, CHUNK)
        return pltpu.make_async_copy(edges_hbm.at[part], edges.at[part], sems.at[chunk])

    @pl.loop(0, (live + CHUNK - 1) // CHUNK)
    def _(chunk):
        load(chunk).start()

    return lambda chunk: load(chunk).wait()


def add_tiles(begin, end, tile_of, product, target, totals):
    @pl.loop(0, (end - begin + GROUP - 1) // GROUP)
    def _(step):
        for k in range(GROUP):
            at = begin + step * GROUP + k
            value = product(tile_of(at).astype(jnp.float32).astype(jnp.bfloat16), at)
            slot = target(at)
            for half, total in enumerate(totals):
                total[slot] += value[:, half * 128 : half * 128 + 128]


def add_chunks(live, wait, tile_of, product, target, totals):
    @pl.loop(0, (live + CHUNK - 1) // CHUNK)
    def _(chunk):
        wait(chunk)
        begin = chunk * CHUNK
        add_tiles(begin, jnp.minimum(live, begin + CHUNK), tile_of, product, target, totals)


def forward_kernel(
    deps, meta_ref, scalars_ref, edges_hbm, own_ref, other_ref, weight_ref, *refs
):
    out_refs = refs[deps : deps + Z]
    panel, left, right, edges, sems = refs[deps + Z :]
    live = scalars_ref[0]
    size = left.shape[1]

    wait = load_all(live, edges_hbm, edges, sems)
    for total in (left, right):
        total[...] = jnp.zeros_like(total)
    for block in range(2 * Y):
        ref, dy = (own_ref, other_ref)[block // Y], block % Y
        scale = scale_of(ref[dy, 2 * size :][:1])
        value = jnp.dot(
            ref[dy, : 2 * size], weight_ref[...], preferred_element_type=jnp.float32
        )
        value = value * jnp.concatenate([scale, scale], axis=1)
        panel[pl.ds(2 * block, 2)] = value.astype(jnp.bfloat16).reshape(2, size, -1)

    def product(tile, at):
        return jnp.dot(tile, panel[meta_ref[COLUMN, at]], preferred_element_type=jnp.float32)

    add_chunks(
        live, wait, lambda at: jnp.where(at < live, edges[at], 0), product,
        lambda at: meta_ref[FORWARD_ROW, at], (left, right),
    )
    for out_ref, dz in zip(out_refs, Z_ORDER):
        for slot in range(2 * X):
            out_ref[slot, :, :128] = left[dz * 2 * X + slot].astype(jnp.bfloat16)
            out_ref[slot, :, 128:] = right[dz * 2 * X + slot].astype(jnp.bfloat16)


def back_product(upstream, tile, slot):
    return lax.dot_general(
        tile, upstream[slot], (((0,), (0,)), ((), ())), preferred_element_type=jnp.float32
    )


def backward_near_kernel(base, places, meta_ref, scalars_ref, edges_hbm, *refs):
    pieces = refs[: len(places)]
    own_hbm, other_hbm, left, right, features_ref, token_ref = refs[len(places) : len(places) + 6]
    own_ref, other_ref, upstream, edges, sems, piece_sems = refs[len(places) + 6 :]
    token_ref[...] = jnp.zeros_like(token_ref)
    live = scalars_ref[0]
    copies = [
        pltpu.make_async_copy(piece, upstream.at[pl.ds(at, piece.shape[0])], piece_sems.at[k])
        for k, (piece, at) in enumerate(zip(pieces, places))
    ]
    for k, (src, dst) in enumerate([(own_hbm, own_ref), (other_hbm, other_ref)], len(places)):
        copies.append(pltpu.make_async_copy(src, dst, piece_sems.at[k]))
    for copy in copies:
        copy.start()
    wait = load_all(live, edges_hbm, edges, sems)
    for total in (left, right):
        total[...] = jnp.zeros_like(total)
    for copy in copies:
        copy.wait()
    nodes = 2 * left.shape[1]
    for block in range(2 * Y):
        ref, dy = (own_ref, other_ref)[block // Y], block % Y
        scale = scale_of(ref[dy, nodes:][:1])
        scaled = ref[dy, :nodes].astype(jnp.float32) * jnp.concatenate([scale, scale], axis=1)
        features_ref[block] = jnp.transpose(scaled).astype(jnp.bfloat16)

    def here(at):
        row = meta_ref[BACK_ROW, at]
        return jnp.logical_and(at < live, jnp.logical_or(row < base, row >= base + 2 * Z))

    add_chunks(
        live, wait, lambda at: jnp.where(here(at), edges[at], 0),
        lambda tile, at: back_product(
            upstream, tile, jnp.where(here(at), meta_ref[BACK_ROW, at], 0)
        ),
        lambda at: meta_ref[COLUMN, at], (left, right),
    )


def backward_far_kernel(
    base, meta_ref, scalars_ref, edges_hbm, piece, near_left, near_right, features_hbm, _,
    back_ref, terms_keep_ref, terms_far_ref,
    left, right, upstream, features_ref, terms, edges, sems, input_sems,
):
    row, count = scalars_ref[1], scalars_ref[2]
    size = left.shape[1]
    pairs = [
        (piece, upstream), (near_left, left), (near_right, right),
        (features_hbm, features_ref),
    ]
    copies = [
        pltpu.make_async_copy(src, dst, input_sems.at[k]) for k, (src, dst) in enumerate(pairs)
    ]

    def load(at):
        return pltpu.make_async_copy(edges_hbm.at[meta_ref[ORDER, at]], edges.at[at], sems.at[at])

    for copy in copies[:3]:
        copy.start()

    @pl.loop(0, count)
    def _(at):
        load(at).start()

    for copy in copies[3:]:
        copy.start()
    for copy in copies[:3]:
        copy.wait()

    @pl.loop(0, count)
    def _(at):
        load(at).wait()

    def number(name, at):
        return meta_ref[name, meta_ref[ORDER, at]]

    add_tiles(
        0, count, lambda at: jnp.where(at < count, edges[at], 0),
        lambda tile, at: back_product(
            upstream, tile, jnp.where(at < count, number(BACK_ROW, at) - base, 0)
        ),
        lambda at: number(COLUMN, at), (left, right),
    )
    for copy in copies[3:]:
        copy.wait()
    y, core = row // 2, row % 2
    result = None
    for block in range(2 * Y):
        far, dy = block // Y, block % Y
        part = pl.ds(2 * block, 2)
        value = jnp.concatenate(
            [
                ref[part].reshape(2 * size, 128) for ref in (left, right)
            ],
            axis=1,
        )
        back_ref[((y + dy) % Y) * 2 + (core + far) % 2] = value.astype(jnp.bfloat16)
        term = jnp.dot(
            features_ref[block], value.astype(jnp.bfloat16), preferred_element_type=jnp.float32
        )
        result = term if result is None else result + term
    terms[...] = result.reshape(terms.shape)
    for block in range(2 * Y):
        far, dy = block // Y, block % Y
        value = terms[((y + dy) % Y) * 2 + (core + far) % 2]
        (terms_far_ref if far else terms_keep_ref)[dy] = value


PARAMS = dict(vmem_limit_bytes=VMEM_MIB * 1024 * 1024)
ANY = pl.BlockSpec(memory_space=pl.ANY)
VMEM = pl.BlockSpec(memory_space=pltpu.VMEM)
SMEM = pl.BlockSpec(memory_space=pltpu.SMEM)


def forward(meta, scalars, edges, own, other, weight, deps=()):
    slots, size, _ = edges.shape
    width = weight.shape[-1]
    f32, bf16 = jnp.float32, jnp.bfloat16
    return pl.pallas_call(
        functools.partial(forward_kernel, len(deps)),
        in_specs=[SMEM, SMEM, ANY, VMEM, VMEM, VMEM] + [ANY] * len(deps),
        out_specs=[VMEM] * Z,
        scratch_shapes=[
            pltpu.VMEM((4 * Y, size, width), bf16),
            pltpu.VMEM((2 * X * Z, size, 128), f32),
            pltpu.VMEM((2 * X * Z, size, 128), f32),
            pltpu.VMEM(edges.shape, edges.dtype),
            pltpu.SemaphoreType.DMA((slots // CHUNK,)),
        ],
        out_shape=[jax.ShapeDtypeStruct((2 * X, size, width), bf16)] * Z,
        compiler_params=pltpu.CompilerParams(**PARAMS),
        cost_estimate=pl.CostEstimate(flops=10**6, bytes_accessed=10**4, transcendentals=0),
        name="forward_tiles",
    )(meta, scalars, edges, own, other, weight, *deps)


def backward_near(meta, scalars, edges, pieces, places, base, own, other):
    slots, size, _ = edges.shape
    width = pieces[0].shape[-1]
    f32, bf16 = jnp.float32, jnp.bfloat16
    return pl.pallas_call(
        functools.partial(backward_near_kernel, base, places),
        in_specs=[SMEM, SMEM, ANY] + [ANY] * (len(pieces) + 2),
        out_specs=[VMEM] * 4,
        scratch_shapes=[
            pltpu.VMEM(own.shape, bf16),
            pltpu.VMEM(other.shape, bf16),
            pltpu.VMEM((2 * X * Z, size, width), bf16),
            pltpu.VMEM(edges.shape, edges.dtype),
            pltpu.SemaphoreType.DMA((slots // CHUNK,)),
            pltpu.SemaphoreType.DMA((len(pieces) + 2,)),
        ],
        out_shape=[jax.ShapeDtypeStruct((4 * Y, size, 128), f32)] * 2
        + [
            jax.ShapeDtypeStruct((2 * Y, width, 2 * size), bf16),
            jax.ShapeDtypeStruct((8, 128), f32),
        ],
        compiler_params=pltpu.CompilerParams(**PARAMS),
        cost_estimate=pl.CostEstimate(flops=10**6, bytes_accessed=10**4, transcendentals=0),
        name="backward_near",
    )(meta, scalars, edges, *pieces, own, other)


def backward_far(meta, scalars, edges, piece, place, left, right, features, after):
    slots, size, _ = edges.shape
    width = piece.shape[-1]
    rows = width // (2 * Y)
    f32, bf16 = jnp.float32, jnp.bfloat16
    outs = [((2 * Y, 2 * size, width), bf16)]
    outs += [((Y, rows, width), f32)] * 2
    return pl.pallas_call(
        functools.partial(backward_far_kernel, place),
        in_specs=[SMEM, SMEM] + [ANY] * 6,
        out_specs=[VMEM] * len(outs),
        scratch_shapes=[
            pltpu.VMEM((4 * Y, size, 128), f32),
            pltpu.VMEM((4 * Y, size, 128), f32),
            pltpu.VMEM(piece.shape, bf16),
            pltpu.VMEM(features.shape, bf16),
            pltpu.VMEM((2 * Y, rows, width), f32),
            pltpu.VMEM(edges.shape, edges.dtype),
            pltpu.SemaphoreType.DMA((slots,)),
            pltpu.SemaphoreType.DMA((4,)),
        ],
        out_shape=[jax.ShapeDtypeStruct(shape, dtype) for shape, dtype in outs],
        compiler_params=pltpu.CompilerParams(**PARAMS),
        cost_estimate=pl.CostEstimate(flops=10**6, bytes_accessed=10**4, transcendentals=0),
        name="backward_far",
    )(meta, scalars, edges, piece, left, right, features, after)


def join_kernel(*refs):
    *parts, out = refs
    for k, part in enumerate(parts):
        out[pl.ds(k * part.shape[0], part.shape[0])] = part[...]


def join(parts, size):
    rows, width = parts[0].shape
    whole = pl.pallas_call(
        join_kernel,
        out_shape=jax.ShapeDtypeStruct((len(parts) * rows, width), parts[0].dtype),
        cost_estimate=pl.CostEstimate(flops=10**6, bytes_accessed=10**4, transcendentals=0),
        name="join",
    )(*parts)
    return whole.reshape(-1, size, width)


def gather_z(own, size, core):
    parts = {0: own}
    up = down = own
    for k in range(1, Z // 2):
        up, down = send(up, "col", along_z(1)), send(down, "col", along_z(-1))
        parts[Z - k], parts[k] = up, down
    parts[Z // 2] = send(jnp.where(core == 0, up, down), ("row", "col"), by_core(along_z))
    return parts[Z // 2 - 1], join([parts[k] for k in range(Z)], size)


def gather_x(plane, core):
    left = send(plane, "col", along_x(1))
    right = send(plane, "col", along_x(-1))
    far = send(jnp.where(core == 0, left, right), ("row", "col"), by_core(along_x))
    return [plane, left, right, far], [0, 3 * 2 * Z, 2 * Z, FAR_X * 2 * Z]


def gather_row(own):
    mine = jnp.stack(
        [
            own,
            send(own, "row", along_y(-1)),
            send(own, "row", along_y(2)),
            send(own, "row", along_y(1)),
        ]
    )
    return mine, send(mine, "row", OTHER_CORE)


def all_rows(value, y, core):
    mine = jnp.stack([value] + [send(value, "row", along_y(d)) for d in range(1, Y)])
    got = jnp.concatenate([mine, send(mine, "row", OTHER_CORE)])
    row = jnp.arange(2 * Y, dtype=jnp.int32)
    order = (row + core) % 2 * Y + (y - row // 2) % Y
    return jnp.take(got, order, axis=0).reshape(-1, value.shape[-1])


def scatter_start(far, first_up, first_down, core):
    f32, bf16 = jnp.float32, jnp.bfloat16
    recv = send(far, ("row", "col"), by_core(along_z)).astype(f32)
    up = (first_up.astype(f32) + jnp.where(core == 0, recv, 0)).astype(bf16)
    down = (first_down.astype(f32) + jnp.where(core == 0, 0, recv)).astype(bf16)
    return up, down


def scatter_round(up, down):
    return send(up, "col", along_z(1)), send(down, "col", along_z(-1))


def fold(received, own):
    return [(b.astype(jnp.float32) + a.astype(jnp.float32)).astype(a.dtype)
            for a, b in zip(received, own)]


def scatter_end(below, above, own):
    f32, bf16 = jnp.float32, jnp.bfloat16
    column = own.astype(f32) + below.astype(f32) + above.astype(f32)
    column = column.reshape(X, -1, column.shape[-1])
    return column[0] + sum(
        send(column[d].astype(bf16), "col", along_x(d)).astype(f32) for d in range(1, X)
    )


def sum_x(value, x):
    got = jnp.stack([value] + [send(value, "col", along_x(d)) for d in range(1, X)])
    order = (x - jnp.arange(X, dtype=jnp.int32)) % X
    return jnp.sum(jnp.take(got, order, axis=0), axis=0)


def sum_z(value):
    for bit in (1, 2, 4):
        value = value + send(value, "col", [(a, a ^ bit) for a in range(X * Z)])
    return value


def shards(features, weight, tile_coords, tile_live, tile_edges, row_degree, col_degree, cotangent):
    f32, bf16 = jnp.float32, jnp.bfloat16
    size = tile_edges.shape[-1]
    nodes, width = features.shape
    row_scale = lax.rsqrt(row_degree.astype(f32))
    col_scale = lax.rsqrt(col_degree.astype(f32))
    coords = tile_coords[0, 0]
    edges = tile_edges[0, 0]
    row, col = lax.axis_index("row"), lax.axis_index("col")
    y, core = row // 2, row % 2

    upstream = (row_scale[:, None] * cotangent.astype(f32)).astype(bf16)
    arrived, plane = gather_z(upstream, size, core)

    degrees = jnp.zeros((16, width), bf16).at[0].set(col_degree.astype(bf16))
    sent, _ = lax.optimization_barrier((jnp.concatenate([features, degrees]), arrived))
    mine, other = gather_row(sent)

    owner, half = coords[:, 0] // 2, coords[:, 0] % 2
    dx = (owner // Z - col // Z) % X
    dz = (owner % Z - col % Z) % Z
    forward_row = (dz * X + dx) * 2 + half
    back_row = (dx * Z + dz) * 2 + half
    col_owner, half = coords[:, 1] // 2, coords[:, 1] % 2
    column = ((col_owner + core) % 2 * Y + (col_owner // 2 - y) % Y) * 2 + half
    live = tile_live[0, 0]
    index = jnp.arange(coords.shape[0], dtype=jnp.int32)
    key = index + 256 * jnp.logical_or(index >= live, dx != FAR_X)
    place = jnp.sum(key[None, :] < key[:, None], axis=1)
    order = jnp.sum(jnp.where(place[:, None] == index, index[:, None], 0), axis=0)
    meta = jnp.stack([forward_row, back_row, column, order]).astype(jnp.int32)
    scalars = jnp.stack([live, row, jnp.sum(key < 256)]).astype(jnp.int32)

    far, *parts = forward(meta, scalars, edges, mine, other, weight)
    (plane, left, right, last), places = gather_x(plane, core)
    up, down = scatter_start(far, *parts[:2], core)
    up, down, left, right = lax.optimization_barrier((up, down, left, right))
    received = scatter_round(up, down)
    *sums, token = backward_near(
        meta, scalars, edges, [plane, left, right], places[:-1], places[-1], mine, other
    )
    up, down = fold(received, parts[2:4])
    up, down, token = lax.optimization_barrier((up, down, token))
    received = scatter_round(up, down)
    back, terms_keep, terms_far = backward_far(
        meta, scalars, edges, last, places[-1], *sums, token
    )
    received = scatter_round(*fold(received, parts[4:6]))
    aggregated = (row_scale[:, None] * scatter_end(*received, parts[6])).astype(bf16)

    terms = terms_keep + send(terms_far, "row", OTHER_CORE)
    terms = terms[0] + sum(send(terms[d], "row", along_y(d)) for d in range(1, Y))
    back = lax.all_to_all(back, "row", 0, 0)
    terms, back = lax.optimization_barrier((sum_z(sum_x(terms, col // Z)), back))
    grad_weight = all_rows(terms, y, core)
    back = jnp.sum(back.astype(f32), axis=0)
    grad_panel = (col_scale[:, None] * back).astype(bf16)
    grad_features = jnp.dot(grad_panel, weight.T, preferred_element_type=f32).astype(bf16)
    return aggregated, grad_features, grad_weight


def solution(mesh):
    in_specs = (
        P(("col", "row"), None),
        P(),
        P("row", "col", None, None),
        P("row", "col"),
        P("row", "col", None, None, None),
        P(("row", "col")),
        P(("col", "row")),
        P(("row", "col"), None),
    )
    out_specs = (P(("row", "col"), None), P(("col", "row"), None), P())
    return jax.shard_map(shards, mesh=mesh, in_specs=in_specs, out_specs=out_specs, check_vma=False)
```
